512 devices in a mesh: dp: 16 (over y, x_lo, core), ctx: 32 (over x_hi, z).
Axes of the slice: x: 4 (x_hi: 2, x_lo: 2; x = x_hi * 2 + x_lo), y: 4, z: 16, core: 2. Of those that a mesh axis runs over, the one named last changes fastest.
Arguments:
- grad_out: bfloat16 [16, 4096, 512], P('dp', 'ctx'), may hold values from -6 to 6
- query_proj: bfloat16 [16, 4096, 512], P('dp', 'ctx'), may hold values from -6 to 6
- key_proj: bfloat16 [16, 4096, 512], P('dp', 'ctx'), may hold values from -6 to 6
- value_proj: bfloat16 [16, 4096, 512], P('dp', 'ctx'), may hold values from -6 to 6
- filters: bfloat16 [512, 4096], P(('ctx', 'dp')), may hold values from -1 to 1
Outputs:
- grad_query: bfloat16 [16, 4096, 512], P('dp', 'ctx')
- grad_key: bfloat16 [16, 4096, 512], P('dp', 'ctx')
- grad_value: bfloat16 [16, 4096, 512], P('dp', 'ctx')
- grad_filters: float32 [512, 4096], P(('ctx', 'dp'))
The draws below stay inside these ranges and needn't reach their ends.
All inputs are finite; a program needn't handle non-finite values.
Results may differ from the reference program's by a relative error of at most 0.022.
Values may be sent and summed in bfloat16 or wider, within the bound.
A program may use at most 64 MiB of HBM per device.

```python
import math
import jax
import jax.numpy as jnp
from jax import lax

SLAB_CHANNELS = 512
SEQS = 16
SEQUENCE_LENGTH = 4096


def draw_filters(key, part):
    key = jax.random.fold_in(key, 7)
    random_key_list = jax.random.split(key, 6)
    delay_offsets = jnp.arange(SEQUENCE_LENGTH, dtype=jnp.float32)
    log_rate = jax.random.uniform(random_key_list[0], (SLAB_CHANNELS, 1), jnp.float32, math.log(0.3 / SEQUENCE_LENGTH), math.log(1.0 / 30.0))
    noise = jnp.clip(jax.random.normal(random_key_list[3], (SLAB_CHANNELS, SEQUENCE_LENGTH), jnp.float32), -3.8, 3.8)
    rate = jnp.exp(log_rate)
    amplitude = jnp.sqrt(jnp.expm1(-2.0 * rate) / jnp.expm1(-2.0 * rate * SEQUENCE_LENGTH))
    spike_position = jax.random.randint(random_key_list[4], (SLAB_CHANNELS, 3), 1, SEQUENCE_LENGTH)
    spike_mask = jax.random.uniform(random_key_list[5], (SLAB_CHANNELS, 3), jnp.float32, 0.5, 0.8)
    decay_profile = jnp.exp(-rate * delay_offsets[None, :])
    for spike_index in range(3):
        arrived_count = delay_offsets[None, :] >= spike_position[:, spike_index:spike_index + 1].astype(jnp.float32)
        decay_profile = decay_profile * jnp.where(arrived_count, spike_mask[:, spike_index:spike_index + 1], 1.0)
    return (amplitude * decay_profile * noise).astype(jnp.bfloat16)


def level_of(key, dims, cuts, smallest, high):
    factor_of = 1.0
    for position, parts in cuts:
        heights = jax.random.uniform(jax.random.fold_in(jax.random.fold_in(key, 6), position), (parts,), jnp.float32, smallest / len(cuts), high / len(cuts))
        factor_of = factor_of * jnp.repeat(jnp.exp(heights), dims[position] // parts).reshape((-1,) + (1,) * (len(dims) - 1 - position))
    return factor_of


def scatter_about(rng, shape, width, limit, pieces=(), held_as=jnp.bfloat16):
    array = width * jax.random.normal(rng, shape, jnp.float32)
    if pieces:
        array = array * level_of(rng, shape, pieces, -0.22, 0.18)
    return jnp.clip(array, -limit, limit).astype(held_as)


def setup_inputs(seed: int = 0) -> dict:
    key_list = jax.random.split(jax.random.key(seed), 6)
    return {
        "grad_out": scatter_about(key_list[0], (SEQS, SEQUENCE_LENGTH, SLAB_CHANNELS), 1.0, 6.0, ((0, 16), (1, 32))),
        "query_proj": scatter_about(key_list[1], (SEQS, SEQUENCE_LENGTH, SLAB_CHANNELS), 1.0, 6.0, ((0, 16), (1, 32))),
        "key_proj": scatter_about(key_list[2], (SEQS, SEQUENCE_LENGTH, SLAB_CHANNELS), 1.0, 6.0, ((0, 16), (1, 32))),
        "value_proj": scatter_about(key_list[3], (SEQS, SEQUENCE_LENGTH, SLAB_CHANNELS), 1.0, 6.0, ((0, 16), (1, 32))),
        "filters": draw_filters(jax.random.fold_in(key_list[5], 71), 0),
    }


def reference(grad_out, query_proj, key_proj, value_proj, filters):
    points = 2 * SEQUENCE_LENGTH
    filter_spec = jnp.fft.rfft(filters.astype(jnp.float32), n=points, axis=1).T

    def one_sequence(running, inputs):
        grad_row, query_row, key_row, value_row = inputs
        grad_conv = (grad_row.astype(jnp.float32) * query_row.astype(jnp.float32)).astype(jnp.bfloat16)
        mixed_in = (key_row.astype(jnp.float32) * value_row.astype(jnp.float32)).astype(jnp.bfloat16)
        mixed_spec = jnp.fft.rfft(mixed_in.astype(jnp.float32), n=points, axis=0)
        grad_spec = jnp.fft.rfft(grad_conv.astype(jnp.float32), n=points, axis=0)
        conv = jnp.fft.irfft(mixed_spec * filter_spec, n=points, axis=0)[:SEQUENCE_LENGTH].astype(jnp.bfloat16)
        back = jnp.fft.irfft(grad_spec * jnp.conj(filter_spec), n=points, axis=0)[:SEQUENCE_LENGTH].astype(jnp.bfloat16)
        lagged = jnp.fft.irfft(grad_spec * jnp.conj(mixed_spec), n=points, axis=0)[:SEQUENCE_LENGTH]
        grad_query = (grad_row.astype(jnp.float32) * conv.astype(jnp.float32)).astype(jnp.bfloat16)
        grad_key = (back.astype(jnp.float32) * value_row.astype(jnp.float32)).astype(jnp.bfloat16)
        grad_value = (back.astype(jnp.float32) * key_row.astype(jnp.float32)).astype(jnp.bfloat16)
        return (running + lagged.T, (grad_query, grad_key, grad_value))
    summed, results = lax.scan(one_sequence, jnp.zeros((SLAB_CHANNELS, SEQUENCE_LENGTH), jnp.float32), (grad_out, query_proj, key_proj, value_proj))
    grad_filters = summed * (1.0 / math.sqrt(SEQS * SEQUENCE_LENGTH))
    return (results[0], results[1], results[2], grad_filters)
```

```python
import functools
import math

import jax
import jax.numpy as jnp
import ml_dtypes
import numpy as np
from jax import lax
from jax.experimental import pallas as pl
from jax.experimental.pallas import tpu as pltpu
from jax.sharding import PartitionSpec as P

MESH = pl.DeviceIdType.MESH
BF16 = ml_dtypes.bfloat16
HALF = 8


def split_table(table):
    high = table.astype(np.float32).astype(BF16)
    low = (table - high.astype(np.float64)).astype(np.float32).astype(BF16)
    return high, low


def make_tables(blocks, width):
    points = blocks * width
    freq = np.arange(blocks) + 0.25
    eye = np.eye(HALF)
    angle_one = 2.0 * np.pi * freq[:, None] * np.arange(blocks)[None, :] / blocks
    cos_one, sin_one = np.cos(angle_one), np.sin(angle_one)

    def spread(block, rows, cols):
        out = block[:, None, :, None] * eye[None, :, None, :]
        if rows == "ck":
            out = out.transpose(1, 0, 2, 3)
        if cols == "ck":
            out = out.transpose(0, 1, 3, 2)
        n = blocks * HALF
        return out.reshape(n, n)

    def first(cols):
        high, low = split_table(
            np.concatenate([spread(cos_one, "kc", cols), spread(-sin_one, "kc", cols)], 0)
        )
        return np.concatenate([high, low], 1)

    def last(rows):
        return split_table(
            np.concatenate([spread(cos_one.T, rows, "kc"), spread(-sin_one.T, rows, "kc")], 1)
            / points
        )

    angle_two = 2.0 * np.pi * (np.arange(width)[:, None] * np.arange(width)[None, :] % width) / width
    cos_two, sin_two = np.cos(angle_two), np.sin(angle_two)
    fwd_high, fwd_low = split_table(np.block([[cos_two, -sin_two], [sin_two, cos_two]]))
    inv_high, inv_low = split_table(np.block([[cos_two, sin_two], [-sin_two, cos_two]]))
    angle_twist = 2.0 * np.pi * freq[:, None] * np.arange(width)[None, :] / points
    twist = np.stack([np.cos(angle_twist), np.sin(angle_twist)])
    twist = np.repeat(twist, HALF, axis=1).astype(np.float32)
    last_tok, last_lag = last("kc"), last("ck")
    return (
        first("kc"),
        first("ck"),
        np.concatenate([fwd_high, fwd_high, fwd_low], 0),
        np.concatenate([inv_high, inv_high, inv_low], 0),
        np.concatenate([last_tok[0], last_tok[0], last_tok[1]], 1),
        np.concatenate([last_lag[0], last_lag[0], last_lag[1]], 1),
        twist,
    )


def dot(a, b):
    return jnp.dot(a, b, preferred_element_type=jnp.float32)


def split(x):
    high = x.astype(jnp.bfloat16)
    low = (x - high.astype(jnp.float32)).astype(jnp.bfloat16)
    return high, low


def forward(signal, first, second, twist):
    n, width = signal.shape[0], signal.shape[1] // 2
    part = dot(first, jnp.concatenate([signal, signal], 0))
    out = []
    for half in range(2):
        lanes = slice(half * width, (half + 1) * width)
        re, im = part[:n, lanes], part[n:, lanes]
        turned = jnp.concatenate(
            [re * twist[0] + im * twist[1], im * twist[0] - re * twist[1]], 1
        )
        high, low = split(turned)
        spec = dot(jnp.concatenate([high, low, high], 1), second)
        out.append((spec[:, :width], spec[:, width:]))
    return out


def inverse(spectra, second, last, twist):
    cols = []
    for re, im in spectra:
        width = re.shape[1]
        high, low = split(jnp.concatenate([re, im], 1))
        rot = dot(jnp.concatenate([high, low, high], 1), second)
        re, im = rot[:, :width], rot[:, width:]
        cols.append(
            jnp.concatenate([re * twist[0] - im * twist[1], im * twist[0] + re * twist[1]], 0)
        )
    high, low = split(jnp.concatenate(cols, 1))
    return dot(last, jnp.concatenate([high, low, high], 0))


def times(a, b):
    return [(ar * br - ai * bi, ar * bi + ai * br) for (ar, ai), (br, bi) in zip(a, b)]


def times_conj(a, b):
    return [(ar * br + ai * bi, ai * br - ar * bi) for (ar, ai), (br, bi) in zip(a, b)]


def pack_tokens(landed):
    blocks, _, width = landed.shape
    wide = landed.astype(jnp.float32)
    sides = [wide[:, h * HALF : (h + 1) * HALF, :].reshape(blocks * HALF, width) for h in range(2)]
    return jnp.concatenate(sides, 1).astype(jnp.bfloat16)


def unpack_tokens(cols, blocks):
    width = cols.shape[1] // 2
    sides = [cols[:, h * width : (h + 1) * width].reshape(blocks, HALF, width) for h in range(2)]
    return jnp.concatenate(sides, 1).astype(jnp.bfloat16)


def ctx_peer(me, step):
    turn = step // 2
    side = (turn + 1) // 2
    along = 8 + side - 2 * side * ((turn + 1) % 2)
    flip = (step + 1) % 2
    return (me // 16 + flip) % 2 * 16 + (me % 16 + along) % 16


def kernel(
    scale,
    go_hbm, q_hbm, k_hbm, v_hbm, f_ref,
    first_tok_hbm, first_filt_hbm, fwd_hbm, inv_hbm, last_tok_hbm, last_lag_hbm, twist_hbm,
    gq_ref, gk_ref, gv_ref, gf_ref,
    go, q, k, v,
    first_tok, first_filt, fwd, inv, last_tok, last_lag, twist,
    g_out, m_out, g_in, m_in, f_wide, f_out, f_in,
    back_out, conv_out, back_in, conv_in, lag_out, lag_in,
    load_sem, table_sem, send_sem, recv_sem,
):
    me, dp = lax.axis_index("ctx"), lax.axis_index("dp")
    n_ctx, n_dp = g_out.shape[0], f_in.shape[0]
    loads = [
        pltpu.make_async_copy(src, dst, load_sem.at[i])
        for i, (src, dst) in enumerate([(go_hbm, go), (q_hbm, q), (k_hbm, k), (v_hbm, v)])
    ]
    for load in loads:
        load.start()
    barrier = pltpu.get_barrier_semaphore()

    def greet_ctx(step, carry):
        pl.semaphore_signal(
            barrier, inc=1, device_id=(dp, ctx_peer(me, step)), device_id_type=MESH
        )
        return carry

    def greet_dp(step, carry):
        pl.semaphore_signal(
            barrier, inc=1, device_id=((dp + step) % n_dp, me), device_id_type=MESH
        )
        return carry

    lax.fori_loop(0, n_ctx - 1, greet_ctx, 0)
    lax.fori_loop(1, n_dp, greet_dp, 0)
    tables = [
        pltpu.make_async_copy(src, dst, table_sem.at[i])
        for i, (src, dst) in enumerate(
            [
                (first_filt_hbm, first_filt),
                (twist_hbm, twist),
                (fwd_hbm, fwd),
                (first_tok_hbm, first_tok),
                (inv_hbm, inv),
                (last_tok_hbm, last_tok),
                (last_lag_hbm, last_lag),
            ]
        )
    ]
    for table in tables:
        table.start()

    def product(a, b):
        wide = a[0].astype(jnp.float32) * b[0].astype(jnp.float32)
        return wide.T.astype(jnp.bfloat16).reshape(g_out.shape)

    loads[0].wait()
    loads[1].wait()
    g_out[...] = product(go, q)
    loads[2].wait()
    loads[3].wait()
    m_out[...] = product(k, v)
    blocks, width = f_out.shape
    row = f_ref[...].astype(jnp.float32)
    for i in range(blocks):
        f_wide[pl.ds(i, 1), :] = row[:, i * width : (i + 1) * width]
    f_out[...] = f_wide[...].astype(jnp.bfloat16)
    pl.semaphore_wait(barrier, n_ctx - 1 + n_dp - 1)

    def send_ctx(src, dst, which):
        def body(step, carry):
            peer = ctx_peer(me, step)
            pltpu.make_async_remote_copy(
                src_ref=src.at[peer],
                dst_ref=dst.at[me],
                send_sem=send_sem.at[which],
                recv_sem=recv_sem.at[which],
                device_id=(dp, peer),
                device_id_type=MESH,
            ).start()
            return carry

        lax.fori_loop(0, n_ctx - 1, body, 0)
        pltpu.make_async_copy(src.at[me], dst.at[me], recv_sem.at[which]).start()

    def send_dp(pick, dst, which):
        def body(step, carry):
            peer = (dp + step) % n_dp
            pltpu.make_async_remote_copy(
                src_ref=pick(peer),
                dst_ref=dst.at[dp],
                send_sem=send_sem.at[which],
                recv_sem=recv_sem.at[which],
                device_id=(peer, me),
                device_id_type=MESH,
            ).start()
            return carry

        lax.fori_loop(1, n_dp, body, 0)
        pltpu.make_async_copy(pick(dp), dst.at[dp], recv_sem.at[which]).start()

    def landed(dst, which):
        pltpu.make_async_copy(dst, dst, recv_sem.at[which]).wait()

    def sent(dst, which):
        rest = dst.at[pl.ds(0, dst.shape[0] - 1)]
        pltpu.make_async_copy(rest, rest, send_sem.at[which]).wait()

    send_ctx(g_out, g_in, 0)
    send_dp(lambda peer: f_out, f_in, 1)
    send_ctx(m_out, m_in, 2)

    for table in tables:
        table.wait()
    landed(f_in, 1)
    filt = jnp.concatenate(
        [f_in[h * HALF : (h + 1) * HALF].reshape(HALF * blocks, width) for h in range(2)], 1
    )
    filt_spec = forward(filt, first_filt[...], fwd[...], twist)
    landed(g_in, 0)
    grad_spec = forward(pack_tokens(g_in[...]), first_tok[...], fwd[...], twist)
    back_cols = inverse(times_conj(grad_spec, filt_spec), inv[...], last_tok[...], twist)
    back_out[...] = unpack_tokens(back_cols, blocks)
    send_ctx(back_out, back_in, 3)
    landed(m_in, 2)
    mixed_spec = forward(pack_tokens(m_in[...]), first_tok[...], fwd[...], twist)
    conv_cols = inverse(times(mixed_spec, filt_spec), inv[...], last_tok[...], twist)
    conv_out[...] = unpack_tokens(conv_cols, blocks)
    send_ctx(conv_out, conv_in, 4)
    lag_cols = inverse(times_conj(grad_spec, mixed_spec), inv[...], last_lag[...], twist)
    for h in range(2):
        lag_out[h * HALF : (h + 1) * HALF] = (
            lag_cols[:, h * width : (h + 1) * width]
            .reshape(HALF, blocks, width)
            .astype(jnp.bfloat16)
        )
    send_dp(lambda peer: lag_out.at[peer], lag_in, 5)

    def rows(arrived):
        wide = arrived[...].astype(jnp.float32).reshape(n_ctx * 2 * HALF, width)
        return wide.T

    landed(back_in, 3)
    back = rows(back_in)
    gk_ref[0] = (back * v[0].astype(jnp.float32)).astype(jnp.bfloat16)
    gv_ref[0] = (back * k[0].astype(jnp.float32)).astype(jnp.bfloat16)
    landed(lag_in, 5)
    gf_ref[...] = jnp.sum(lag_in[...].astype(jnp.float32), axis=0) * scale
    landed(conv_in, 4)
    gq_ref[0] = (rows(conv_in) * go[0].astype(jnp.float32)).astype(jnp.bfloat16)
    for which, dst in enumerate([g_in, f_in, m_in, back_in, conv_in, lag_in]):
        sent(dst, which)


def per_device(grad_out, query_proj, key_proj, value_proj, filters):
    n_ctx, n_dp = lax.axis_size("ctx"), lax.axis_size("dp")
    _, width, channels = grad_out.shape
    blocks = n_ctx
    own = channels // n_ctx
    assert own == n_dp == 2 * HALF and filters.shape == (1, blocks * width)
    tables = make_tables(blocks, width)
    scale = 1.0 / math.sqrt(grad_out.shape[0] * n_dp * n_ctx * width)
    vmem = pl.BlockSpec(memory_space=pltpu.VMEM)
    hbm = pl.BlockSpec(memory_space=pl.ANY)
    bf16, f32 = jnp.bfloat16, jnp.float32
    tok = grad_out.shape
    cols = pltpu.VMEM((n_ctx, own, width), bf16)
    rows = pltpu.VMEM((n_dp, blocks, width), bf16)
    outs = pl.pallas_call(
        functools.partial(kernel, scale),
        out_shape=[
            jax.ShapeDtypeStruct(tok, bf16),
            jax.ShapeDtypeStruct(tok, bf16),
            jax.ShapeDtypeStruct(tok, bf16),
            jax.ShapeDtypeStruct((blocks, width), f32),
        ],
        in_specs=[hbm] * 4 + [vmem] + [hbm] * len(tables),
        out_specs=[vmem] * 4,
        scratch_shapes=[pltpu.VMEM(tok, bf16)] * 4
        + [pltpu.VMEM(t.shape, t.dtype) for t in tables]
        + [cols] * 4
        + [pltpu.VMEM((blocks, width), f32), pltpu.VMEM((blocks, width), bf16), rows]
        + [cols] * 4
        + [rows] * 2
        + [
            pltpu.SemaphoreType.DMA((4,)),
            pltpu.SemaphoreType.DMA((len(tables),)),
            pltpu.SemaphoreType.DMA((6,)),
            pltpu.SemaphoreType.DMA((6,)),
        ],
        compiler_params=pltpu.CompilerParams(
            collective_id=0, has_side_effects=True, vmem_limit_bytes=40 * 1024 * 1024
        ),
        name="hyena_backward",
    )(grad_out, query_proj, key_proj, value_proj, filters, *[jnp.asarray(t) for t in tables])
    return (*outs[:3], outs[3].reshape(filters.shape))


def solution(mesh):
    tokens, channels = P("dp", "ctx", None), P(("ctx", "dp"), None)
    return jax.shard_map(
        per_device,
        mesh=mesh,
        in_specs=(tokens, tokens, tokens, tokens, channels),
        out_specs=(tokens, tokens, tokens, channels),
        check_vma=False,
    )
```

```python
import functools
import math

import jax
import jax.numpy as jnp
import ml_dtypes
import numpy as np
from jax import lax
from jax.experimental import pallas as pl
from jax.experimental.pallas import tpu as pltpu
from jax.sharding import PartitionSpec as P

MESH = pl.DeviceIdType.MESH
BF16 = ml_dtypes.bfloat16
HALF = 8


def split_table(table):
    high = table.astype(np.float32).astype(BF16)
    low = (table - high.astype(np.float64)).astype(np.float32).astype(BF16)
    return high, low


def make_tables(blocks, width):
    points = blocks * width
    freq = np.arange(blocks) + 0.25
    eye = np.eye(HALF)
    angle_one = 2.0 * np.pi * freq[:, None] * np.arange(blocks)[None, :] / blocks
    cos_one, sin_one = np.cos(angle_one), np.sin(angle_one)

    def spread(block, rows, cols):
        out = block[:, None, :, None] * eye[None, :, None, :]
        if rows == "ck":
            out = out.transpose(1, 0, 2, 3)
        if cols == "ck":
            out = out.transpose(0, 1, 3, 2)
        n = blocks * HALF
        return out.reshape(n, n)

    def first(cols):
        high, low = split_table(
            np.concatenate([spread(cos_one, "kc", cols), spread(-sin_one, "kc", cols)], 0)
        )
        return np.concatenate([high, low], 1)

    def last(rows):
        return split_table(
            np.concatenate([spread(cos_one.T, rows, "kc"), spread(-sin_one.T, rows, "kc")], 1)
            / points
        )

    angle_two = 2.0 * np.pi * (np.arange(width)[:, None] * np.arange(width)[None, :] % width) / width
    cos_two, sin_two = np.cos(angle_two), np.sin(angle_two)
    fwd_high, fwd_low = split_table(np.block([[cos_two, -sin_two], [sin_two, cos_two]]))
    inv_high, inv_low = split_table(np.block([[cos_two, sin_two], [-sin_two, cos_two]]))
    angle_twist = 2.0 * np.pi * freq[:, None] * np.arange(width)[None, :] / points
    twist = np.stack([np.cos(angle_twist), np.sin(angle_twist)])
    twist = np.repeat(twist, HALF, axis=1).astype(np.float32)
    last_tok, last_lag = last("kc"), last("ck")
    return (
        first("kc"),
        first("ck"),
        np.concatenate([fwd_high, fwd_high, fwd_low], 0),
        np.concatenate([inv_high, inv_high, inv_low], 0),
        np.concatenate([last_tok[0], last_tok[0], last_tok[1]], 1),
        np.concatenate([last_lag[0], last_lag[0], last_lag[1]], 1),
        twist,
    )


def dot(a, b):
    return jnp.dot(a, b, preferred_element_type=jnp.float32)


def split(x):
    high = x.astype(jnp.bfloat16)
    low = (x - high.astype(jnp.float32)).astype(jnp.bfloat16)
    return high, low


def forward(signal, first, second, twist):
    n, width = signal.shape[0], signal.shape[1] // 2
    part = dot(first, jnp.concatenate([signal, signal], 0))
    out = []
    for half in range(2):
        lanes = slice(half * width, (half + 1) * width)
        re, im = part[:n, lanes], part[n:, lanes]
        turned = jnp.concatenate(
            [re * twist[0] + im * twist[1], im * twist[0] - re * twist[1]], 1
        )
        high, low = split(turned)
        spec = dot(jnp.concatenate([high, low, high], 1), second)
        out.append((spec[:, :width], spec[:, width:]))
    return out


def inverse(spectra, second, last, twist):
    cols = []
    for re, im in spectra:
        width = re.shape[1]
        high, low = split(jnp.concatenate([re, im], 1))
        rot = dot(jnp.concatenate([high, low, high], 1), second)
        re, im = rot[:, :width], rot[:, width:]
        cols.append(
            jnp.concatenate([re * twist[0] - im * twist[1], im * twist[0] + re * twist[1]], 0)
        )
    high, low = split(jnp.concatenate(cols, 1))
    return dot(last, jnp.concatenate([high, low, high], 0))


def times(a, b):
    return [(ar * br - ai * bi, ar * bi + ai * br) for (ar, ai), (br, bi) in zip(a, b)]


def times_conj(a, b):
    return [(ar * br + ai * bi, ai * br - ar * bi) for (ar, ai), (br, bi) in zip(a, b)]


def pack_tokens(landed):
    blocks, _, width = landed.shape
    wide = landed.astype(jnp.float32)
    sides = [wide[:, h * HALF : (h + 1) * HALF, :].reshape(blocks * HALF, width) for h in range(2)]
    return jnp.concatenate(sides, 1).astype(jnp.bfloat16)


def unpack_tokens(cols, blocks):
    width = cols.shape[1] // 2
    sides = [cols[:, h * width : (h + 1) * width].reshape(blocks, HALF, width) for h in range(2)]
    return jnp.concatenate(sides, 1).astype(jnp.bfloat16)


def ctx_peer(me, step):
    turn = step // 2
    side = (turn + 1) // 2
    along = 8 + side - 2 * side * ((turn + 1) % 2)
    flip = (step + 1) % 2
    return (me // 16 + flip) % 2 * 16 + (me % 16 + along) % 16


def kernel(
    scale,
    go_hbm, q_hbm, k_hbm, v_hbm, f_hbm,
    first_tok_hbm, first_filt_hbm, fwd_hbm, inv_hbm, last_tok_hbm, last_lag_hbm, twist_hbm,
    gq_ref, gk_ref, gf_ref,
    go, q, k, v, f_row,
    first_tok, first_filt, fwd, inv, last_tok, last_lag, twist,
    g_out, m_out, g_in, m_in, f_wide, f_out, f_in,
    back_out, conv_out, back_in, conv_in, lag_out, lag_in,
    load_sem, table_sem, send_sem, recv_sem,
):
    me, dp = lax.axis_index("ctx"), lax.axis_index("dp")
    n_ctx, n_dp = g_out.shape[0], f_in.shape[0]
    loads = [
        pltpu.make_async_copy(src, dst, load_sem.at[i])
        for i, (src, dst) in enumerate([(go_hbm, go), (q_hbm, q), (k_hbm, k), (v_hbm, v), (f_hbm, f_row)])
    ]
    for load in loads:
        load.start()
    barrier = pltpu.get_barrier_semaphore()

    def greet_ctx(step, carry):
        pl.semaphore_signal(
            barrier, inc=1, device_id=(dp, ctx_peer(me, step)), device_id_type=MESH
        )
        return carry

    def greet_dp(step, carry):
        pl.semaphore_signal(
            barrier, inc=1, device_id=((dp + step) % n_dp, me), device_id_type=MESH
        )
        return carry

    lax.fori_loop(0, n_ctx - 1, greet_ctx, 0, unroll=True)
    lax.fori_loop(1, n_dp, greet_dp, 0, unroll=True)
    tables = [
        pltpu.make_async_copy(src, dst, table_sem.at[i])
        for i, (src, dst) in enumerate(
            [
                (first_filt_hbm, first_filt),
                (twist_hbm, twist),
                (fwd_hbm, fwd),
                (first_tok_hbm, first_tok),
                (inv_hbm, inv),
                (last_tok_hbm, last_tok),
                (last_lag_hbm, last_lag),
            ]
        )
    ]
    for table in tables:
        table.start()

    def product(a, b):
        wide = a[0].astype(jnp.float32) * b[0].astype(jnp.float32)
        return wide.T.astype(jnp.bfloat16).reshape(g_out.shape)

    loads[0].wait()
    loads[1].wait()
    g_out[...] = product(go, q)
    loads[2].wait()
    loads[3].wait()
    m_out[...] = product(k, v)
    blocks, width = f_out.shape
    loads[4].wait()
    row = f_row[...].astype(jnp.float32)
    for i in range(blocks):
        f_wide[pl.ds(i, 1), :] = row[:, i * width : (i + 1) * width]
    f_out[...] = f_wide[...].astype(jnp.bfloat16)
    pl.semaphore_wait(barrier, n_ctx - 1 + n_dp - 1)

    def send_ctx(src, dst, which):
        def body(step, carry):
            peer = ctx_peer(me, step)
            pltpu.make_async_remote_copy(
                src_ref=src.at[peer],
                dst_ref=dst.at[me],
                send_sem=send_sem.at[which],
                recv_sem=recv_sem.at[which],
                device_id=(dp, peer),
                device_id_type=MESH,
            ).start()
            return carry

        lax.fori_loop(0, n_ctx - 1, body, 0, unroll=True)
        pltpu.make_async_copy(src.at[me], dst.at[me], recv_sem.at[which]).start()

    def send_dp(pick, dst, which):
        def body(step, carry):
            peer = (dp + step) % n_dp
            pltpu.make_async_remote_copy(
                src_ref=pick(peer),
                dst_ref=dst.at[dp],
                send_sem=send_sem.at[which],
                recv_sem=recv_sem.at[which],
                device_id=(peer, me),
                device_id_type=MESH,
            ).start()
            return carry

        lax.fori_loop(1, n_dp, body, 0, unroll=True)
        pltpu.make_async_copy(pick(dp), dst.at[dp], recv_sem.at[which]).start()

    def landed(dst, which):
        pltpu.make_async_copy(dst, dst, recv_sem.at[which]).wait()

    def sent(dst, which):
        rest = dst.at[pl.ds(0, dst.shape[0] - 1)]
        pltpu.make_async_copy(rest, rest, send_sem.at[which]).wait()

    send_ctx(g_out, g_in, 0)
    send_dp(lambda peer: f_out, f_in, 1)
    send_ctx(m_out, m_in, 2)

    for table in tables:
        table.wait()
    landed(f_in, 1)
    filt = jnp.concatenate(
        [f_in[h * HALF : (h + 1) * HALF].reshape(HALF * blocks, width) for h in range(2)], 1
    )
    filt_spec = forward(filt, first_filt[...], fwd[...], twist)
    landed(g_in, 0)
    grad_spec = forward(pack_tokens(g_in[...]), first_tok[...], fwd[...], twist)
    back_cols = inverse(times_conj(grad_spec, filt_spec), inv[...], last_tok[...], twist)
    back_out[...] = unpack_tokens(back_cols, blocks)
    send_ctx(back_out, back_in, 3)
    landed(m_in, 2)
    mixed_spec = forward(pack_tokens(m_in[...]), first_tok[...], fwd[...], twist)
    conv_cols = inverse(times(mixed_spec, filt_spec), inv[...], last_tok[...], twist)
    conv_out[...] = unpack_tokens(conv_cols, blocks)
    send_ctx(conv_out, conv_in, 4)
    lag_cols = inverse(times_conj(grad_spec, mixed_spec), inv[...], last_lag[...], twist)
    for h in range(2):
        lag_out[h * HALF : (h + 1) * HALF] = (
            lag_cols[:, h * width : (h + 1) * width]
            .reshape(HALF, blocks, width)
            .astype(jnp.bfloat16)
        )
    send_dp(lambda peer: lag_out.at[peer], lag_in, 5)

    def rows(arrived):
        wide = arrived[...].astype(jnp.float32).reshape(n_ctx * 2 * HALF, width)
        return wide.T

    landed(back_in, 3)
    back = rows(back_in)
    gk_ref[0] = back.astype(jnp.bfloat16)
    landed(lag_in, 5)
    gf_ref[...] = jnp.sum(lag_in[...].astype(jnp.float32), axis=0) * scale
    landed(conv_in, 4)
    gq_ref[0] = rows(conv_in).astype(jnp.bfloat16)
    for which, dst in enumerate([g_in, f_in, m_in, back_in, conv_in, lag_in]):
        sent(dst, which)


def per_device(grad_out, query_proj, key_proj, value_proj, filters):
    n_ctx, n_dp = lax.axis_size("ctx"), lax.axis_size("dp")
    _, width, channels = grad_out.shape
    blocks = n_ctx
    own = channels // n_ctx
    assert own == n_dp == 2 * HALF and filters.shape == (1, blocks * width)
    tables = make_tables(blocks, width)
    scale = 1.0 / math.sqrt(grad_out.shape[0] * n_dp * n_ctx * width)
    vmem = pl.BlockSpec(memory_space=pltpu.VMEM)
    hbm = pl.BlockSpec(memory_space=pltpu.HBM)
    bf16, f32 = jnp.bfloat16, jnp.float32
    tok = grad_out.shape
    cols = pltpu.VMEM((n_ctx, own, width), bf16)
    rows = pltpu.VMEM((n_dp, blocks, width), bf16)
    outs = pl.pallas_call(
        functools.partial(kernel, scale),
        out_shape=[
            jax.ShapeDtypeStruct(tok, bf16),
            jax.ShapeDtypeStruct(tok, bf16),
            jax.ShapeDtypeStruct((blocks, width), f32),
        ],
        in_specs=[hbm] * (5 + len(tables)),
        out_specs=[vmem] * 3,
        scratch_shapes=[pltpu.VMEM(tok, bf16)] * 4
        + [pltpu.VMEM(filters.shape, bf16)]
        + [pltpu.VMEM(t.shape, t.dtype) for t in tables]
        + [cols] * 4
        + [pltpu.VMEM((blocks, width), f32), pltpu.VMEM((blocks, width), bf16), rows]
        + [cols] * 4
        + [rows] * 2
        + [
            pltpu.SemaphoreType.DMA((5,)),
            pltpu.SemaphoreType.DMA((len(tables),)),
            pltpu.SemaphoreType.DMA((6,)),
            pltpu.SemaphoreType.DMA((6,)),
        ],
        compiler_params=pltpu.CompilerParams(
            collective_id=0, has_side_effects=True, vmem_limit_bytes=63 * 1024 * 1024
        ),
        name="hyena_backward",
    )(grad_out, query_proj, key_proj, value_proj, filters, *[jnp.asarray(t) for t in tables])
    wide = lambda x: x.astype(f32)
    conv, back = wide(outs[0]), wide(outs[1])
    return ((conv*wide(grad_out)).astype(bf16),(back*wide(value_proj)).astype(bf16),(back*wide(key_proj)).astype(bf16), outs[2].reshape(filters.shape))


def solution(mesh):
    tokens, channels = P("dp", "ctx", None), P(("ctx", "dp"), None)
    return jax.shard_map(
        per_device,
        mesh=mesh,
        in_specs=(tokens, tokens, tokens, tokens, channels),
        out_specs=(tokens, tokens, tokens, channels),
        check_vma=False,
    )
```

```python
import functools
import math

import jax
import jax.numpy as jnp
import ml_dtypes
import numpy as np
from jax import lax
from jax.experimental import pallas as pl
from jax.experimental.pallas import tpu as pltpu
from jax.sharding import PartitionSpec as P

MESH = pl.DeviceIdType.MESH
BF16 = ml_dtypes.bfloat16
HALF = 8
ROW = 16


def split_table(table):
    high = table.astype(np.float32).astype(BF16)
    low = (table - high.astype(np.float64)).astype(np.float32).astype(BF16)
    return high, low


def make_tables(blocks, width):
    points = blocks * width
    freq = np.arange(blocks) + 0.25
    eye = np.eye(HALF)
    angle_one = 2.0 * np.pi * freq[:, None] * np.arange(blocks)[None, :] / blocks
    cos_one, sin_one = np.cos(angle_one), np.sin(angle_one)

    def spread(block, rows, cols):
        out = block[:, None, :, None] * eye[None, :, None, :]
        if rows == "ck":
            out = out.transpose(1, 0, 2, 3)
        if cols == "ck":
            out = out.transpose(0, 1, 3, 2)
        n = blocks * HALF
        return out.reshape(n, n)

    def first(cols):
        high, low = split_table(
            np.concatenate([spread(cos_one, "kc", cols), spread(-sin_one, "kc", cols)], 0)
        )
        return np.concatenate([high, low], 1)

    def last(rows):
        return split_table(
            np.concatenate([spread(cos_one.T, rows, "kc"), spread(-sin_one.T, rows, "kc")], 1)
            / points
        )

    angle_two = 2.0 * np.pi * (np.arange(width)[:, None] * np.arange(width)[None, :] % width) / width
    cos_two, sin_two = np.cos(angle_two), np.sin(angle_two)
    fwd_high, fwd_low = split_table(np.block([[cos_two, -sin_two], [sin_two, cos_two]]))
    inv_high, inv_low = split_table(np.block([[cos_two, sin_two], [-sin_two, cos_two]]))
    angle_twist = 2.0 * np.pi * freq[:, None] * np.arange(width)[None, :] / points
    twist = np.stack([np.cos(angle_twist), np.sin(angle_twist)])
    twist = np.repeat(twist, HALF, axis=1).astype(np.float32)
    last_tok, last_lag = last("kc"), last("ck")
    return (
        first("kc"),
        first("ck"),
        np.concatenate([fwd_high, fwd_high, fwd_low], 0),
        np.concatenate([inv_high, inv_high, inv_low], 0),
        np.concatenate([last_tok[0], last_tok[0], last_tok[1]], 1),
        np.concatenate([last_lag[0], last_lag[0], last_lag[1]], 1),
        twist,
    )


def dot(a, b):
    return jnp.dot(a, b, preferred_element_type=jnp.float32)


def split(x):
    high = x.astype(jnp.bfloat16)
    low = (x - high.astype(jnp.float32)).astype(jnp.bfloat16)
    return high, low


def forward(signal, first, second, twist):
    n, width = signal.shape[0], signal.shape[1] // 2
    part = dot(first, jnp.concatenate([signal, signal], 0))
    out = []
    for half in range(2):
        lanes = slice(half * width, (half + 1) * width)
        re, im = part[:n, lanes], part[n:, lanes]
        turned = jnp.concatenate(
            [re * twist[0] + im * twist[1], im * twist[0] - re * twist[1]], 1
        )
        high, low = split(turned)
        spec = dot(jnp.concatenate([high, low, high], 1), second)
        out.append((spec[:, :width], spec[:, width:]))
    return out


def inverse(spectra, second, last, twist):
    cols = []
    for re, im in spectra:
        width = re.shape[1]
        high, low = split(jnp.concatenate([re, im], 1))
        rot = dot(jnp.concatenate([high, low, high], 1), second)
        re, im = rot[:, :width], rot[:, width:]
        cols.append(
            jnp.concatenate([re * twist[0] - im * twist[1], im * twist[0] + re * twist[1]], 0)
        )
    high, low = split(jnp.concatenate(cols, 1))
    return dot(last, jnp.concatenate([high, low, high], 0))


def times(a, b):
    return [(ar * br - ai * bi, ar * bi + ai * br) for (ar, ai), (br, bi) in zip(a, b)]


def times_conj(a, b):
    return [(ar * br + ai * bi, ai * br - ar * bi) for (ar, ai), (br, bi) in zip(a, b)]


def pack_tokens(landed):
    blocks, _, width = landed.shape
    wide = landed.astype(jnp.float32)
    sides = [wide[:, h * HALF : (h + 1) * HALF, :].reshape(blocks * HALF, width) for h in range(2)]
    return jnp.concatenate(sides, 1).astype(jnp.bfloat16)


def unpack_tokens(cols, blocks):
    width = cols.shape[1] // 2
    sides = [cols[:, h * width : (h + 1) * width].reshape(blocks, HALF, width) for h in range(2)]
    return jnp.concatenate(sides, 1).astype(jnp.bfloat16)


def along(me, step):
    side = (step + 1) // 2
    return (me + 8 + side - 2 * side * ((step + 1) % 2)) % ROW


def kernel(
    go_hbm, q_hbm, k_hbm, v_hbm, f_hbm,
    first_tok_hbm, first_filt_hbm, fwd_hbm, inv_hbm, last_tok_hbm, last_lag_hbm, twist_hbm,
    conv_in, back_in, lag_in,
    go, q, k, v, f_row,
    first_tok, first_filt, fwd, inv, last_tok, last_lag, twist,
    g_out, m_out, g_in, m_in, f_wide, f_out, f_in,
    back_out, conv_out, lag_out,
    load_sem, table_sem, send_sem, recv_sem, row_sem,
):
    me, dp = lax.axis_index("ctx"), lax.axis_index("dp")
    n_ctx, n_dp = g_out.shape[0], f_in.shape[0]
    loads = [
        pltpu.make_async_copy(src, dst, load_sem.at[i])
        for i, (src, dst) in enumerate([(go_hbm, go), (q_hbm, q), (k_hbm, k), (v_hbm, v), (f_hbm, f_row)])
    ]
    for load in loads:
        load.start()
    barrier = pltpu.get_barrier_semaphore()

    row = me // ROW

    def greet(sem, z, x):
        pl.semaphore_signal(sem, inc=1, device_id=(dp, x * ROW + z), device_id_type=MESH)

    for step in range(ROW - 1):
        greet(barrier, along(me, step), row)

    @pl.when(row == 0)
    def _():
        for step in range(ROW):
            greet(barrier, along(me, step), 1)

    for step in range(1, n_dp):
        pl.semaphore_signal(
            barrier, inc=1, device_id=((dp + step) % n_dp, me), device_id_type=MESH
        )
    tables = [
        pltpu.make_async_copy(src, dst, table_sem.at[i])
        for i, (src, dst) in enumerate(
            [
                (first_filt_hbm, first_filt),
                (twist_hbm, twist),
                (fwd_hbm, fwd),
                (first_tok_hbm, first_tok),
                (inv_hbm, inv),
                (last_tok_hbm, last_tok),
                (last_lag_hbm, last_lag),
            ]
        )
    ]
    for table in tables:
        table.start()

    def product(a, b):
        wide = a[0].astype(jnp.float32) * b[0].astype(jnp.float32)
        return wide.T.astype(jnp.bfloat16).reshape(g_out.shape)

    loads[0].wait()
    loads[1].wait()
    g_out[...] = product(go, q)
    loads[2].wait()
    loads[3].wait()
    m_out[...] = product(k, v)
    blocks, width = f_out.shape
    loads[4].wait()
    taps = f_row[...].astype(jnp.float32)
    for i in range(blocks):
        f_wide[pl.ds(i, 1), :] = taps[:, i * width : (i + 1) * width]
    f_out[...] = f_wide[...].astype(jnp.bfloat16)
    pl.semaphore_wait(barrier, ROW - 1 + n_dp - 1 + ROW * row)

    @pl.when(row == 1)
    def _():
        greet(row_sem, me % ROW, 0)

    def send_one(src, dst, which, to, z):
        peer = to * ROW + z
        pltpu.make_async_remote_copy(
            src_ref=src.at[peer],
            dst_ref=dst.at[me],
            send_sem=send_sem.at[which],
            recv_sem=recv_sem.at[which],
            device_id=(dp, peer),
            device_id_type=MESH,
        ).start()

    def send_same(src, dst, which):
        for step in range(ROW - 1):
            send_one(src, dst, which, row, along(me, step))

    def send_cross(src, dst, which):
        for step in range(ROW):
            send_one(src, dst, which, 1 - row, along(me, step))

    def send_both(src, dst, which, first=1):
        for step in range(ROW):
            for flip in (first, 1 - first):
                if flip or step < ROW - 1:
                    send_one(src, dst, which, (row + flip) % 2, along(me, step))

    def keep(src, dst, which):
        pltpu.make_async_copy(src.at[me], dst.at[me], recv_sem.at[which]).start()

    def send_dp(pick, dst, which):
        def body(step, carry):
            peer = (dp + step) % n_dp
            pltpu.make_async_remote_copy(
                src_ref=pick(peer),
                dst_ref=dst.at[dp],
                send_sem=send_sem.at[which],
                recv_sem=recv_sem.at[which],
                device_id=(peer, me),
                device_id_type=MESH,
            ).start()
            return carry

        lax.fori_loop(1, n_dp, body, 0, unroll=True)
        pltpu.make_async_copy(pick(dp), dst.at[dp], recv_sem.at[which]).start()

    def landed(dst, which):
        pltpu.make_async_copy(dst, dst, recv_sem.at[which]).wait()

    def sent(dst, which):
        rest = dst.at[pl.ds(0, dst.shape[0] - 1)]
        pltpu.make_async_copy(rest, rest, send_sem.at[which]).wait()

    keep(g_out, g_in, 0)
    keep(m_out, m_in, 2)

    @pl.when(row == 0)
    def _():
        send_same(g_out, g_in, 0)
        pl.semaphore_wait(row_sem, 1)
        send_cross(g_out, g_in, 0)
        send_both(m_out, m_in, 2)

    @pl.when(row == 1)
    def _():
        send_both(g_out, g_in, 0)
        send_both(m_out, m_in, 2)

    send_dp(lambda peer: f_out, f_in, 1)
    for table in tables:
        table.wait()
    landed(f_in, 1)
    filt = jnp.concatenate(
        [f_in[h * HALF : (h + 1) * HALF].reshape(HALF * blocks, width) for h in range(2)], 1
    )
    filt_spec = forward(filt, first_filt[...], fwd[...], twist)
    landed(g_in, 0)
    grad_spec = forward(pack_tokens(g_in[...]), first_tok[...], fwd[...], twist)
    back_cols = inverse(times_conj(grad_spec, filt_spec), inv[...], last_tok[...], twist)
    back_out[...] = unpack_tokens(back_cols, blocks)
    keep(back_out, back_in, 3)
    send_both(back_out, back_in, 3)
    landed(m_in, 2)
    mixed_spec = forward(pack_tokens(m_in[...]), first_tok[...], fwd[...], twist)
    conv_cols = inverse(times(mixed_spec, filt_spec), inv[...], last_tok[...], twist)
    conv_out[...] = unpack_tokens(conv_cols, blocks)
    keep(conv_out, conv_in, 4)

    @pl.when(row == 0)
    def _():
        send_both(conv_out, conv_in, 4)

    @pl.when(row == 1)
    def _():
        send_cross(conv_out, conv_in, 4)
        send_same(conv_out, conv_in, 4)
    lag_cols = inverse(times_conj(grad_spec, mixed_spec), inv[...], last_lag[...], twist)
    for h in range(2):
        lag_out[h * HALF : (h + 1) * HALF] = (
            lag_cols[:, h * width : (h + 1) * width]
            .reshape(HALF, blocks, width)
            .astype(jnp.bfloat16)
        )
    send_dp(lambda peer: lag_out.at[peer], lag_in, 5)

    landed(back_in, 3)
    landed(lag_in, 5)
    landed(conv_in, 4)
    for which, dst in enumerate([g_in, f_in, m_in, back_in, conv_in, lag_in]):
        sent(dst, which)


def gate(scale, conv, back, lag, go, k, v, gq_ref, gk_ref, gv_ref, gf_ref):
    channels, width = go.shape[2], go.shape[1]

    def rows(arrived):
        return arrived[...].astype(jnp.float32).reshape(channels, width).T

    cols = rows(back)
    gk_ref[0] = (cols * v[0].astype(jnp.float32)).astype(jnp.bfloat16)
    gv_ref[0] = (cols * k[0].astype(jnp.float32)).astype(jnp.bfloat16)
    gq_ref[0] = (rows(conv) * go[0].astype(jnp.float32)).astype(jnp.bfloat16)
    gf_ref[...] = jnp.sum(lag[...].astype(jnp.float32), axis=0) * scale


def per_device(grad_out, query_proj, key_proj, value_proj, filters):
    n_ctx, n_dp = lax.axis_size("ctx"), lax.axis_size("dp")
    _, width, channels = grad_out.shape
    blocks = n_ctx
    own = channels // n_ctx
    assert own == n_dp == 2 * HALF and filters.shape == (1, blocks * width)
    tables = make_tables(blocks, width)
    scale = 1.0 / math.sqrt(grad_out.shape[0] * n_dp * n_ctx * width)
    vmem = pl.BlockSpec(memory_space=pltpu.VMEM)
    hbm = pl.BlockSpec(memory_space=pltpu.HBM)
    bf16, f32 = jnp.bfloat16, jnp.float32
    tok = grad_out.shape
    cols = pltpu.VMEM((n_ctx, own, width), bf16)
    rows = pltpu.VMEM((n_dp, blocks, width), bf16)
    outs = pl.pallas_call(
        kernel,
        out_shape=[
            jax.ShapeDtypeStruct((n_ctx, own, width), bf16),
            jax.ShapeDtypeStruct((n_ctx, own, width), bf16),
            jax.ShapeDtypeStruct((n_dp, blocks, width), bf16),
        ],
        in_specs=[hbm] * (5 + len(tables)),
        out_specs=[hbm] * 3,
        scratch_shapes=[pltpu.VMEM(tok, bf16)] * 4
        + [pltpu.VMEM(filters.shape, bf16)]
        + [pltpu.VMEM(t.shape, t.dtype) for t in tables]
        + [cols] * 4
        + [pltpu.VMEM((blocks, width), f32), pltpu.VMEM((blocks, width), bf16), rows]
        + [cols] * 2
        + [rows]
        + [
            pltpu.SemaphoreType.DMA((5,)),
            pltpu.SemaphoreType.DMA((len(tables),)),
            pltpu.SemaphoreType.DMA((6,)),
            pltpu.SemaphoreType.DMA((6,)),
            pltpu.SemaphoreType.REGULAR,
        ],
        compiler_params=pltpu.CompilerParams(
            collective_id=0, has_side_effects=True, vmem_limit_bytes=63 * 1024 * 1024
        ),
        name="hyena_backward",
    )(grad_out, query_proj, key_proj, value_proj, filters, *[jnp.asarray(t) for t in tables])
    outs = pl.pallas_call(
        functools.partial(gate, scale),
        out_shape=[jax.ShapeDtypeStruct(tok, bf16)] * 3
        + [jax.ShapeDtypeStruct((blocks, width), f32)],
        in_specs=[vmem] * 6,
        out_specs=[vmem] * 4,
        compiler_params=pltpu.CompilerParams(vmem_limit_bytes=63 * 1024 * 1024),
        name="gate_outputs",
    )(outs[0], outs[1], outs[2], grad_out, key_proj, value_proj)
    return (*outs[:3], outs[3].reshape(filters.shape))


def solution(mesh):
    tokens, channels = P("dp", "ctx", None), P(("ctx", "dp"), None)
    return jax.shard_map(
        per_device,
        mesh=mesh,
        in_specs=(tokens, tokens, tokens, tokens, channels),
        out_specs=(tokens, tokens, tokens, channels),
        check_vma=False,
    )
```

```python
import functools
import math

import jax
import jax.numpy as jnp
import ml_dtypes
import numpy as np
from jax import lax
from jax.experimental import pallas as pl
from jax.experimental.pallas import tpu as pltpu
from jax.sharding import PartitionSpec as P

MESH = pl.DeviceIdType.MESH
BF16 = ml_dtypes.bfloat16
HALF = 8
ROW = 16


def split_table(table):
    high = table.astype(np.float32).astype(BF16)
    low = (table - high.astype(np.float64)).astype(np.float32).astype(BF16)
    return high, low


def make_tables(blocks, width):
    points = blocks * width
    freq = np.arange(blocks) + 0.25
    eye = np.eye(HALF)
    angle_one = 2.0 * np.pi * freq[:, None] * np.arange(blocks)[None, :] / blocks
    cos_one, sin_one = np.cos(angle_one), np.sin(angle_one)

    def spread(block, rows, cols):
        out = block[:, None, :, None] * eye[None, :, None, :]
        if rows == "ck":
            out = out.transpose(1, 0, 2, 3)
        if cols == "ck":
            out = out.transpose(0, 1, 3, 2)
        n = blocks * HALF
        return out.reshape(n, n)

    def first(cols):
        high, low = split_table(
            np.concatenate([spread(cos_one, "kc", cols), spread(-sin_one, "kc", cols)], 0)
        )
        return np.concatenate([high, low], 1)

    def last(rows):
        return split_table(
            np.concatenate([spread(cos_one.T, rows, "kc"), spread(-sin_one.T, rows, "kc")], 1)
            / points
        )

    angle_two = 2.0 * np.pi * (np.arange(width)[:, None] * np.arange(width)[None, :] % width) / width
    cos_two, sin_two = np.cos(angle_two), np.sin(angle_two)
    fwd_high, fwd_low = split_table(np.block([[cos_two, -sin_two], [sin_two, cos_two]]))
    inv_high, inv_low = split_table(np.block([[cos_two, sin_two], [-sin_two, cos_two]]))
    angle_twist = 2.0 * np.pi * freq[:, None] * np.arange(width)[None, :] / points
    twist = np.stack([np.cos(angle_twist), np.sin(angle_twist)])
    twist = np.repeat(twist, HALF, axis=1).astype(np.float32)
    last_tok, last_lag = last("kc"), last("ck")
    return (
        first("kc"),
        first("ck"),
        np.concatenate([fwd_high, fwd_high, fwd_low], 0),
        np.concatenate([inv_high, inv_high, inv_low], 0),
        np.concatenate([last_tok[0], last_tok[0], last_tok[1]], 1),
        np.concatenate([last_lag[0], last_lag[0], last_lag[1]], 1),
        twist,
    )


def dot(a, b):
    return jnp.dot(a, b, preferred_element_type=jnp.float32)


def split(x):
    high = x.astype(jnp.bfloat16)
    low = (x - high.astype(jnp.float32)).astype(jnp.bfloat16)
    return high, low


def forward(signal, first, second, twist):
    n, width = signal.shape[0], signal.shape[1] // 2
    part = dot(first, jnp.concatenate([signal, signal], 0))
    out = []
    for half in range(2):
        lanes = slice(half * width, (half + 1) * width)
        re, im = part[:n, lanes], part[n:, lanes]
        turned = jnp.concatenate(
            [re * twist[0] + im * twist[1], im * twist[0] - re * twist[1]], 1
        )
        high, low = split(turned)
        spec = dot(jnp.concatenate([high, low, high], 1), second)
        out.append((spec[:, :width], spec[:, width:]))
    return out


def inverse(spectra, second, last, twist):
    cols = []
    for re, im in spectra:
        width = re.shape[1]
        high, low = split(jnp.concatenate([re, im], 1))
        rot = dot(jnp.concatenate([high, low, high], 1), second)
        re, im = rot[:, :width], rot[:, width:]
        cols.append(
            jnp.concatenate([re * twist[0] - im * twist[1], im * twist[0] + re * twist[1]], 0)
        )
    high, low = split(jnp.concatenate(cols, 1))
    return dot(last, jnp.concatenate([high, low, high], 0))


def times(a, b):
    return [(ar * br - ai * bi, ar * bi + ai * br) for (ar, ai), (br, bi) in zip(a, b)]


def times_conj(a, b):
    return [(ar * br + ai * bi, ai * br - ar * bi) for (ar, ai), (br, bi) in zip(a, b)]


def pack_tokens(landed):
    blocks, _, width = landed.shape
    wide = landed.astype(jnp.float32)
    sides = [wide[:, h * HALF : (h + 1) * HALF, :].reshape(blocks * HALF, width) for h in range(2)]
    return jnp.concatenate(sides, 1).astype(jnp.bfloat16)


def unpack_tokens(cols, blocks):
    width = cols.shape[1] // 2
    sides = [cols[:, h * width : (h + 1) * width].reshape(blocks, HALF, width) for h in range(2)]
    return jnp.concatenate(sides, 1).astype(jnp.bfloat16)


def along(me, step):
    side = (step + 1) // 2
    return (me + 8 + side - 2 * side * ((step + 1) % 2)) % ROW


def kernel(
    go_hbm, q_hbm, k_hbm, v_hbm, f_hbm,
    first_tok_hbm, first_filt_hbm, fwd_hbm, inv_hbm, last_tok_hbm, last_lag_hbm, twist_hbm,
    conv_in, back_in, lag_in,
    go, q, k, v, f_row,
    first_tok, first_filt, fwd, inv, last_tok, last_lag, twist,
    g_out, m_out, g_in, m_in, f_wide, f_out, f_in,
    back_out, conv_out, lag_out,
    load_sem, table_sem, send_sem, recv_sem, row_sem,
):
    me, dp = lax.axis_index("ctx"), lax.axis_index("dp")
    n_ctx, n_dp = g_out.shape[0], f_in.shape[0]
    loads = [
        pltpu.make_async_copy(src, dst, load_sem.at[i])
        for i, (src, dst) in enumerate([(go_hbm, go), (q_hbm, q), (k_hbm, k), (v_hbm, v), (f_hbm, f_row)])
    ]
    for load in loads:
        load.start()
    barrier = pltpu.get_barrier_semaphore()

    row = me // ROW

    def greet(sem, z, x):
        pl.semaphore_signal(sem, inc=1, device_id=(dp, x * ROW + z), device_id_type=MESH)

    for step in range(ROW - 1):
        greet(barrier, along(me, step), row)

    for step in range(1, n_dp):
        pl.semaphore_signal(
            barrier, inc=1, device_id=((dp + step) % n_dp, me), device_id_type=MESH
        )
    tables = [
        pltpu.make_async_copy(src, dst, table_sem.at[i])
        for i, (src, dst) in enumerate(
            [
                (first_filt_hbm, first_filt),
                (twist_hbm, twist),
                (fwd_hbm, fwd),
                (first_tok_hbm, first_tok),
                (inv_hbm, inv),
                (last_tok_hbm, last_tok),
                (last_lag_hbm, last_lag),
            ]
        )
    ]
    for table in tables:
        table.start()

    def product(a, b):
        wide = a[0].astype(jnp.float32) * b[0].astype(jnp.float32)
        return wide.T.astype(jnp.bfloat16).reshape(g_out.shape)

    loads[0].wait()
    loads[1].wait()
    g_out[...] = product(go, q)
    loads[2].wait()
    loads[3].wait()
    m_out[...] = product(k, v)
    blocks, width = f_out.shape
    loads[4].wait()
    taps = f_row[...].astype(jnp.float32)
    for i in range(blocks):
        f_wide[pl.ds(i, 1), :] = taps[:, i * width : (i + 1) * width]
    f_out[...] = f_wide[...].astype(jnp.bfloat16)
    pl.semaphore_wait(barrier, ROW - 1 + n_dp - 1 + row)

    @pl.when(row == 0)
    def _():
        greet(barrier, me % ROW, 1)

    @pl.when(row == 1)
    def _():
        greet(row_sem, me % ROW, 0)

    def send_one(src, dst, which, to, z):
        peer = to * ROW + z
        pltpu.make_async_remote_copy(
            src_ref=src.at[peer],
            dst_ref=dst.at[me],
            send_sem=send_sem.at[which],
            recv_sem=recv_sem.at[which],
            device_id=(dp, peer),
            device_id_type=MESH,
        ).start()

    def send_same(src, dst, which):
        for step in range(ROW - 1):
            send_one(src, dst, which, row, along(me, step))

    def send_cross(src, dst, which):
        for step in range(ROW):
            send_one(src, dst, which, 1 - row, along(me, step))

    def send_both(src, dst, which, first=1):
        for step in range(ROW):
            for flip in (first, 1 - first):
                if flip or step < ROW - 1:
                    send_one(src, dst, which, (row + flip) % 2, along(me, step))

    def keep(src, dst, which):
        pltpu.make_async_copy(src.at[me], dst.at[me], recv_sem.at[which]).start()

    def send_dp(pick, dst, which):
        def body(step, carry):
            peer = (dp + step) % n_dp
            pltpu.make_async_remote_copy(
                src_ref=pick(peer),
                dst_ref=dst.at[dp],
                send_sem=send_sem.at[which],
                recv_sem=recv_sem.at[which],
                device_id=(peer, me),
                device_id_type=MESH,
            ).start()
            return carry

        lax.fori_loop(1, n_dp, body, 0, unroll=True)
        pltpu.make_async_copy(pick(dp), dst.at[dp], recv_sem.at[which]).start()

    def landed(dst, which):
        pltpu.make_async_copy(dst, dst, recv_sem.at[which]).wait()

    def sent(dst, which):
        rest = dst.at[pl.ds(0, dst.shape[0] - 1)]
        pltpu.make_async_copy(rest, rest, send_sem.at[which]).wait()

    keep(g_out, g_in, 0)
    keep(m_out, m_in, 2)

    @pl.when(row == 0)
    def _():
        send_same(g_out, g_in, 0)
        pl.semaphore_wait(row_sem, 1)
        send_cross(g_out, g_in, 0)
        send_both(m_out, m_in, 2)

    @pl.when(row == 1)
    def _():
        send_cross(g_out, g_in, 0)
        send_same(g_out, g_in, 0)
        send_both(m_out, m_in, 2)

    send_dp(lambda peer: f_out, f_in, 1)
    for table in tables:
        table.wait()
    landed(f_in, 1)
    filt = jnp.concatenate(
        [f_in[h * HALF : (h + 1) * HALF].reshape(HALF * blocks, width) for h in range(2)], 1
    )
    filt_spec = forward(filt, first_filt[...], fwd[...], twist)
    landed(g_in, 0)
    grad_spec = forward(pack_tokens(g_in[...]), first_tok[...], fwd[...], twist)
    back_cols = inverse(times_conj(grad_spec, filt_spec), inv[...], last_tok[...], twist)
    back_out[...] = unpack_tokens(back_cols, blocks)
    keep(back_out, back_in, 3)
    send_both(back_out, back_in, 3)
    landed(m_in, 2)
    mixed_spec = forward(pack_tokens(m_in[...]), first_tok[...], fwd[...], twist)
    conv_cols = inverse(times(mixed_spec, filt_spec), inv[...], last_tok[...], twist)
    conv_out[...] = unpack_tokens(conv_cols, blocks)
    keep(conv_out, conv_in, 4)

    @pl.when(row == 0)
    def _():
        send_both(conv_out, conv_in, 4)

    @pl.when(row == 1)
    def _():
        send_cross(conv_out, conv_in, 4)
        send_same(conv_out, conv_in, 4)
    lag_cols = inverse(times_conj(grad_spec, mixed_spec), inv[...], last_lag[...], twist)
    for h in range(2):
        lag_out[h * HALF : (h + 1) * HALF] = (
            lag_cols[:, h * width : (h + 1) * width]
            .reshape(HALF, blocks, width)
            .astype(jnp.bfloat16)
        )
    send_dp(lambda peer: lag_out.at[peer], lag_in, 5)

    landed(back_in, 3)
    landed(lag_in, 5)
    landed(conv_in, 4)
    for which, dst in enumerate([g_in, f_in, m_in, back_in, conv_in, lag_in]):
        sent(dst, which)


def gate(scale, conv, back, lag, go, k, v, gq_ref, gk_ref, gv_ref, gf_ref):
    channels, width = go.shape[2], go.shape[1]

    def rows(arrived):
        return arrived[...].astype(jnp.float32).reshape(channels, width).T

    cols = rows(back)
    gk_ref[0] = (cols * v[0].astype(jnp.float32)).astype(jnp.bfloat16)
    gv_ref[0] = (cols * k[0].astype(jnp.float32)).astype(jnp.bfloat16)
    gq_ref[0] = (rows(conv) * go[0].astype(jnp.float32)).astype(jnp.bfloat16)
    gf_ref[...] = jnp.sum(lag[...].astype(jnp.float32), axis=0) * scale


def per_device(grad_out, query_proj, key_proj, value_proj, filters):
    n_ctx, n_dp = lax.axis_size("ctx"), lax.axis_size("dp")
    _, width, channels = grad_out.shape
    blocks = n_ctx
    own = channels // n_ctx
    assert own == n_dp == 2 * HALF and filters.shape == (1, blocks * width)
    tables = make_tables(blocks, width)
    scale = 1.0 / math.sqrt(grad_out.shape[0] * n_dp * n_ctx * width)
    vmem = pl.BlockSpec(memory_space=pltpu.VMEM)
    hbm = pl.BlockSpec(memory_space=pltpu.HBM)
    bf16, f32 = jnp.bfloat16, jnp.float32
    tok = grad_out.shape
    cols = pltpu.VMEM((n_ctx, own, width), bf16)
    rows = pltpu.VMEM((n_dp, blocks, width), bf16)
    outs = pl.pallas_call(
        kernel,
        out_shape=[
            jax.ShapeDtypeStruct((n_ctx, own, width), bf16),
            jax.ShapeDtypeStruct((n_ctx, own, width), bf16),
            jax.ShapeDtypeStruct((n_dp, blocks, width), bf16),
        ],
        in_specs=[hbm] * (5 + len(tables)),
        out_specs=[hbm] * 3,
        scratch_shapes=[pltpu.VMEM(tok, bf16)] * 4
        + [pltpu.VMEM(filters.shape, bf16)]
        + [pltpu.VMEM(t.shape, t.dtype) for t in tables]
        + [cols] * 4
        + [pltpu.VMEM((blocks, width), f32), pltpu.VMEM((blocks, width), bf16), rows]
        + [cols] * 2
        + [rows]
        + [
            pltpu.SemaphoreType.DMA((5,)),
            pltpu.SemaphoreType.DMA((len(tables),)),
            pltpu.SemaphoreType.DMA((6,)),
            pltpu.SemaphoreType.DMA((6,)),
            pltpu.SemaphoreType.REGULAR,
        ],
        compiler_params=pltpu.CompilerParams(
            collective_id=0, has_side_effects=True, vmem_limit_bytes=63 * 1024 * 1024
        ),
        name="hyena_backward",
    )(grad_out, query_proj, key_proj, value_proj, filters, *[jnp.asarray(t) for t in tables])
    outs = pl.pallas_call(
        functools.partial(gate, scale),
        out_shape=[jax.ShapeDtypeStruct(tok, bf16)] * 3
        + [jax.ShapeDtypeStruct((blocks, width), f32)],
        in_specs=[vmem] * 6,
        out_specs=[vmem] * 4,
        compiler_params=pltpu.CompilerParams(vmem_limit_bytes=63 * 1024 * 1024),
        name="gate_outputs",
    )(outs[0], outs[1], outs[2], grad_out, key_proj, value_proj)
    return (*outs[:3], outs[3].reshape(filters.shape))


def solution(mesh):
    tokens, channels = P("dp", "ctx", None), P(("ctx", "dp"), None)
    return jax.shard_map(
        per_device,
        mesh=mesh,
        in_specs=(tokens, tokens, tokens, tokens, channels),
        out_specs=(tokens, tokens, tokens, channels),
        check_vma=False,
    )
```

```python
import functools
import math

import jax
import jax.numpy as jnp
import ml_dtypes
import numpy as np
from jax import lax
from jax.experimental import pallas as pl
from jax.experimental.pallas import tpu as pltpu
from jax.sharding import PartitionSpec as P

MESH = pl.DeviceIdType.MESH
BF16 = ml_dtypes.bfloat16
HALF = 8
ROW = 16


def split_table(table):
    high = table.astype(np.float32).astype(BF16)
    low = (table - high.astype(np.float64)).astype(np.float32).astype(BF16)
    return high, low


def make_tables(blocks, width):
    points = blocks * width
    freq = np.arange(blocks) + 0.25
    eye = np.eye(HALF)
    angle_one = 2.0 * np.pi * freq[:, None] * np.arange(blocks)[None, :] / blocks
    cos_one, sin_one = np.cos(angle_one), np.sin(angle_one)

    def spread(block, rows, cols):
        out = block[:, None, :, None] * eye[None, :, None, :]
        if rows == "ck":
            out = out.transpose(1, 0, 2, 3)
        if cols == "ck":
            out = out.transpose(0, 1, 3, 2)
        n = blocks * HALF
        return out.reshape(n, n)

    def first(cols):
        high, low = split_table(
            np.concatenate([spread(cos_one, "kc", cols), spread(-sin_one, "kc", cols)], 0)
        )
        return np.concatenate([high, low], 1)

    def last(rows):
        return split_table(
            np.concatenate([spread(cos_one.T, rows, "kc"), spread(-sin_one.T, rows, "kc")], 1)
            / points
        )

    angle_two = 2.0 * np.pi * (np.arange(width)[:, None] * np.arange(width)[None, :] % width) / width
    cos_two, sin_two = np.cos(angle_two), np.sin(angle_two)
    fwd_high, fwd_low = split_table(np.block([[cos_two, -sin_two], [sin_two, cos_two]]))
    inv_high, inv_low = split_table(np.block([[cos_two, sin_two], [-sin_two, cos_two]]))
    angle_twist = 2.0 * np.pi * freq[:, None] * np.arange(width)[None, :] / points
    twist = np.stack([np.cos(angle_twist), np.sin(angle_twist)])
    twist = np.repeat(twist, HALF, axis=1).astype(np.float32)
    last_tok, last_lag = last("kc"), last("ck")
    return (
        first("kc"),
        first("ck"),
        np.concatenate([fwd_high, fwd_high, fwd_low], 0),
        np.concatenate([inv_high, inv_high, inv_low], 0),
        np.concatenate([last_tok[0], last_tok[0], last_tok[1]], 1),
        np.concatenate([last_lag[0], last_lag[0], last_lag[1]], 1),
        twist,
    )


def dot(a, b):
    return jnp.dot(a, b, preferred_element_type=jnp.float32)


def split(x):
    high = x.astype(jnp.bfloat16)
    low = (x - high.astype(jnp.float32)).astype(jnp.bfloat16)
    return high, low


def forward(signal, first, second, twist):
    n, width = signal.shape[0], signal.shape[1] // 2
    part = dot(first, jnp.concatenate([signal, signal], 0))
    out = []
    for half in range(2):
        lanes = slice(half * width, (half + 1) * width)
        re, im = part[:n, lanes], part[n:, lanes]
        turned = jnp.concatenate(
            [re * twist[0] + im * twist[1], im * twist[0] - re * twist[1]], 1
        )
        high, low = split(turned)
        spec = dot(jnp.concatenate([high, low, high], 1), second)
        out.append((spec[:, :width], spec[:, width:]))
    return out


def inverse(spectra, second, last, twist):
    cols = []
    for re, im in spectra:
        width = re.shape[1]
        high, low = split(jnp.concatenate([re, im], 1))
        rot = dot(jnp.concatenate([high, low, high], 1), second)
        re, im = rot[:, :width], rot[:, width:]
        cols.append(
            jnp.concatenate([re * twist[0] - im * twist[1], im * twist[0] + re * twist[1]], 0)
        )
    high, low = split(jnp.concatenate(cols, 1))
    return dot(last, jnp.concatenate([high, low, high], 0))


def times(a, b):
    return [(ar * br - ai * bi, ar * bi + ai * br) for (ar, ai), (br, bi) in zip(a, b)]


def times_conj(a, b):
    return [(ar * br + ai * bi, ai * br - ar * bi) for (ar, ai), (br, bi) in zip(a, b)]


def pack_tokens(landed):
    blocks, _, width = landed.shape
    wide = landed.astype(jnp.float32)
    sides = [wide[:, h * HALF : (h + 1) * HALF, :].reshape(blocks * HALF, width) for h in range(2)]
    return jnp.concatenate(sides, 1).astype(jnp.bfloat16)


def unpack_tokens(cols, blocks):
    width = cols.shape[1] // 2
    sides = [cols[:, h * width : (h + 1) * width].reshape(blocks, HALF, width) for h in range(2)]
    return jnp.concatenate(sides, 1).astype(jnp.bfloat16)


def along(me, step):
    side = (step + 1) // 2
    return (me + 8 + side - 2 * side * ((step + 1) % 2)) % ROW


def kernel(
    go_hbm, q_hbm, k_hbm, v_hbm, f_hbm,
    first_tok_hbm, first_filt_hbm, fwd_hbm, inv_hbm, last_tok_hbm, last_lag_hbm, twist_hbm,
    conv_in, back_in, lag_in,
    go, q, k, v, f_row,
    first_tok, first_filt, fwd, inv, last_tok, last_lag, twist,
    g_out, m_out, g_in, m_in, f_wide, f_out, f_in,
    back_out, conv_out, lag_out,
    load_sem, table_sem, send_sem, recv_sem, row_sem,
):
    me, dp = lax.axis_index("ctx"), lax.axis_index("dp")
    n_ctx, n_dp = g_out.shape[0], f_in.shape[0]
    loads = [
        pltpu.make_async_copy(src, dst, load_sem.at[i])
        for i, (src, dst) in enumerate([(go_hbm, go), (q_hbm, q), (k_hbm, k), (v_hbm, v), (f_hbm, f_row)])
    ]
    barrier = pltpu.get_barrier_semaphore()

    row = me // ROW

    def greet(sem, z, x):
        pl.semaphore_signal(sem, inc=1, device_id=(dp, x * ROW + z), device_id_type=MESH)

    for step in range(ROW - 1):
        greet(barrier, along(me, step), row)

    for step in range(1, n_dp):
        pl.semaphore_signal(
            barrier, inc=1, device_id=((dp + step) % n_dp, me), device_id_type=MESH
        )
    for load in loads:
        load.start()
    tables = [
        pltpu.make_async_copy(src, dst, table_sem.at[i])
        for i, (src, dst) in enumerate(
            [
                (first_filt_hbm, first_filt),
                (twist_hbm, twist),
                (fwd_hbm, fwd),
                (first_tok_hbm, first_tok),
                (inv_hbm, inv),
                (last_tok_hbm, last_tok),
                (last_lag_hbm, last_lag),
            ]
        )
    ]
    for table in tables:
        table.start()

    def product(a, b):
        wide = a[0].astype(jnp.float32) * b[0].astype(jnp.float32)
        return wide.T.astype(jnp.bfloat16).reshape(g_out.shape)

    loads[0].wait()
    loads[1].wait()
    g_out[...] = product(go, q)
    blocks, width = f_out.shape
    pl.semaphore_wait(barrier, ROW - 1 + n_dp - 1 + row)

    @pl.when(row == 0)
    def _():
        greet(barrier, me % ROW, 1)

    @pl.when(row == 1)
    def _():
        greet(row_sem, me % ROW, 0)

    def send_one(src, dst, which, to, z):
        peer = to * ROW + z
        pltpu.make_async_remote_copy(
            src_ref=src.at[peer],
            dst_ref=dst.at[me],
            send_sem=send_sem.at[which],
            recv_sem=recv_sem.at[which],
            device_id=(dp, peer),
            device_id_type=MESH,
        ).start()

    def send_same(src, dst, which):
        for step in range(ROW - 1):
            send_one(src, dst, which, row, along(me, step))

    def send_cross(src, dst, which):
        for step in range(ROW):
            send_one(src, dst, which, 1 - row, along(me, step))

    def send_both(src, dst, which, first=1):
        for step in range(ROW):
            for flip in (first, 1 - first):
                if flip or step < ROW - 1:
                    send_one(src, dst, which, (row + flip) % 2, along(me, step))

    def keep(src, dst, which):
        pltpu.make_async_copy(src.at[me], dst.at[me], recv_sem.at[which]).start()

    def send_dp(pick, dst, which):
        def body(step, carry):
            peer = (dp + step) % n_dp
            pltpu.make_async_remote_copy(
                src_ref=pick(peer),
                dst_ref=dst.at[dp],
                send_sem=send_sem.at[which],
                recv_sem=recv_sem.at[which],
                device_id=(peer, me),
                device_id_type=MESH,
            ).start()
            return carry

        lax.fori_loop(1, n_dp, body, 0, unroll=True)
        pltpu.make_async_copy(pick(dp), dst.at[dp], recv_sem.at[which]).start()

    def landed(dst, which):
        pltpu.make_async_copy(dst, dst, recv_sem.at[which]).wait()

    def sent(dst, which):
        rest = dst.at[pl.ds(0, dst.shape[0] - 1)]
        pltpu.make_async_copy(rest, rest, send_sem.at[which]).wait()

    keep(g_out, g_in, 0)

    @pl.when(row == 0)
    def _():
        send_same(g_out, g_in, 0)
        pl.semaphore_wait(row_sem, 1)
        send_cross(g_out, g_in, 0)

    @pl.when(row == 1)
    def _():
        send_cross(g_out, g_in, 0)
        send_same(g_out, g_in, 0)

    loads[2].wait()
    loads[3].wait()
    m_out[...] = product(k, v)
    keep(m_out, m_in, 2)
    send_both(m_out, m_in, 2)
    loads[4].wait()
    taps = f_row[...].astype(jnp.float32)
    for i in range(blocks):
        f_wide[pl.ds(i, 1), :] = taps[:, i * width : (i + 1) * width]
    f_out[...] = f_wide[...].astype(jnp.bfloat16)
    send_dp(lambda peer: f_out, f_in, 1)
    for table in tables:
        table.wait()
    landed(f_in, 1)
    filt = jnp.concatenate(
        [f_in[h * HALF : (h + 1) * HALF].reshape(HALF * blocks, width) for h in range(2)], 1
    )
    filt_spec = forward(filt, first_filt[...], fwd[...], twist)
    landed(g_in, 0)
    grad_spec = forward(pack_tokens(g_in[...]), first_tok[...], fwd[...], twist)
    back_cols = inverse(times_conj(grad_spec, filt_spec), inv[...], last_tok[...], twist)
    back_out[...] = unpack_tokens(back_cols, blocks)
    keep(back_out, back_in, 3)
    send_both(back_out, back_in, 3)
    landed(m_in, 2)
    mixed_spec = forward(pack_tokens(m_in[...]), first_tok[...], fwd[...], twist)
    conv_cols = inverse(times(mixed_spec, filt_spec), inv[...], last_tok[...], twist)
    conv_out[...] = unpack_tokens(conv_cols, blocks)
    keep(conv_out, conv_in, 4)

    @pl.when(row == 0)
    def _():
        send_both(conv_out, conv_in, 4)

    @pl.when(row == 1)
    def _():
        send_cross(conv_out, conv_in, 4)
        send_same(conv_out, conv_in, 4)
    lag_cols = inverse(times_conj(grad_spec, mixed_spec), inv[...], last_lag[...], twist)
    for h in range(2):
        lag_out[h * HALF : (h + 1) * HALF] = (
            lag_cols[:, h * width : (h + 1) * width]
            .reshape(HALF, blocks, width)
            .astype(jnp.bfloat16)
        )
    send_dp(lambda peer: lag_out.at[peer], lag_in, 5)

    landed(back_in, 3)
    landed(lag_in, 5)
    landed(conv_in, 4)
    for which, dst in enumerate([g_in, f_in, m_in, back_in, conv_in, lag_in]):
        sent(dst, which)


def gate(scale, conv, back, lag, go, k, v, gq_ref, gk_ref, gv_ref, gf_ref):
    channels, width = go.shape[2], go.shape[1]

    def rows(arrived):
        return arrived[...].astype(jnp.float32).reshape(channels, width).T

    cols = rows(back)
    gk_ref[0] = (cols * v[0].astype(jnp.float32)).astype(jnp.bfloat16)
    gv_ref[0] = (cols * k[0].astype(jnp.float32)).astype(jnp.bfloat16)
    gq_ref[0] = (rows(conv) * go[0].astype(jnp.float32)).astype(jnp.bfloat16)
    gf_ref[...] = jnp.sum(lag[...].astype(jnp.float32), axis=0) * scale


def per_device(grad_out, query_proj, key_proj, value_proj, filters):
    n_ctx, n_dp = lax.axis_size("ctx"), lax.axis_size("dp")
    _, width, channels = grad_out.shape
    blocks = n_ctx
    own = channels // n_ctx
    assert own == n_dp == 2 * HALF and filters.shape == (1, blocks * width)
    tables = make_tables(blocks, width)
    scale = 1.0 / math.sqrt(grad_out.shape[0] * n_dp * n_ctx * width)
    vmem = pl.BlockSpec(memory_space=pltpu.VMEM)
    hbm = pl.BlockSpec(memory_space=pltpu.HBM)
    bf16, f32 = jnp.bfloat16, jnp.float32
    tok = grad_out.shape
    cols = pltpu.VMEM((n_ctx, own, width), bf16)
    rows = pltpu.VMEM((n_dp, blocks, width), bf16)
    outs = pl.pallas_call(
        kernel,
        out_shape=[
            jax.ShapeDtypeStruct((n_ctx, own, width), bf16),
            jax.ShapeDtypeStruct((n_ctx, own, width), bf16),
            jax.ShapeDtypeStruct((n_dp, blocks, width), bf16),
        ],
        in_specs=[hbm] * (5 + len(tables)),
        out_specs=[hbm] * 3,
        scratch_shapes=[pltpu.VMEM(tok, bf16)] * 4
        + [pltpu.VMEM(filters.shape, bf16)]
        + [pltpu.VMEM(t.shape, t.dtype) for t in tables]
        + [cols] * 4
        + [pltpu.VMEM((blocks, width), f32), pltpu.VMEM((blocks, width), bf16), rows]
        + [cols] * 2
        + [rows]
        + [
            pltpu.SemaphoreType.DMA((5,)),
            pltpu.SemaphoreType.DMA((len(tables),)),
            pltpu.SemaphoreType.DMA((6,)),
            pltpu.SemaphoreType.DMA((6,)),
            pltpu.SemaphoreType.REGULAR,
        ],
        compiler_params=pltpu.CompilerParams(
            collective_id=0, has_side_effects=True, vmem_limit_bytes=63 * 1024 * 1024
        ),
        name="hyena_backward",
    )(grad_out, query_proj, key_proj, value_proj, filters, *[jnp.asarray(t) for t in tables])
    outs = pl.pallas_call(
        functools.partial(gate, scale),
        out_shape=[jax.ShapeDtypeStruct(tok, bf16)] * 3
        + [jax.ShapeDtypeStruct((blocks, width), f32)],
        in_specs=[vmem] * 6,
        out_specs=[vmem] * 4,
        compiler_params=pltpu.CompilerParams(vmem_limit_bytes=63 * 1024 * 1024),
        name="gate_outputs",
    )(outs[0], outs[1], outs[2], grad_out, key_proj, value_proj)
    return (*outs[:3], outs[3].reshape(filters.shape))


def solution(mesh):
    tokens, channels = P("dp", "ctx", None), P(("ctx", "dp"), None)
    return jax.shard_map(
        per_device,
        mesh=mesh,
        in_specs=(tokens, tokens, tokens, tokens, channels),
        out_specs=(tokens, tokens, tokens, channels),
        check_vma=False,
    )
```

```python
import functools
import math

import jax
import jax.numpy as jnp
import ml_dtypes
import numpy as np
from jax import lax
from jax.experimental import pallas as pl
from jax.experimental.pallas import tpu as pltpu
from jax.sharding import PartitionSpec as P

MESH = pl.DeviceIdType.MESH
BF16 = ml_dtypes.bfloat16
HALF = 8
ROW = 16


def split_table(table):
    high = table.astype(np.float32).astype(BF16)
    low = (table - high.astype(np.float64)).astype(np.float32).astype(BF16)
    return high, low


def make_tables(blocks, width):
    points = blocks * width
    freq = np.arange(blocks) + 0.25
    eye = np.eye(HALF)
    angle_one = 2.0 * np.pi * freq[:, None] * np.arange(blocks)[None, :] / blocks
    cos_one, sin_one = np.cos(angle_one), np.sin(angle_one)

    def spread(block, rows, cols):
        out = block[:, None, :, None] * eye[None, :, None, :]
        if rows == "ck":
            out = out.transpose(1, 0, 2, 3)
        if cols == "ck":
            out = out.transpose(0, 1, 3, 2)
        n = blocks * HALF
        return out.reshape(n, n)

    def first(cols):
        high, low = split_table(
            np.concatenate([spread(cos_one, "kc", cols), spread(-sin_one, "kc", cols)], 0)
        )
        return np.concatenate([high, low], 1)

    def last(rows):
        return split_table(
            np.concatenate([spread(cos_one.T, rows, "kc"), spread(-sin_one.T, rows, "kc")], 1)
            / points
        )

    angle_two = 2.0 * np.pi * (np.arange(width)[:, None] * np.arange(width)[None, :] % width) / width
    cos_two, sin_two = np.cos(angle_two), np.sin(angle_two)
    fwd_high, fwd_low = split_table(np.block([[cos_two, -sin_two], [sin_two, cos_two]]))
    inv_high, inv_low = split_table(np.block([[cos_two, sin_two], [-sin_two, cos_two]]))
    angle_twist = 2.0 * np.pi * freq[:, None] * np.arange(width)[None, :] / points
    twist = np.stack([np.cos(angle_twist), np.sin(angle_twist)])
    twist = np.repeat(twist, HALF, axis=1).astype(np.float32)
    last_tok, last_lag = last("kc"), last("ck")
    return (
        first("kc"),
        first("ck"),
        np.concatenate([fwd_high, fwd_high, fwd_low], 0),
        np.concatenate([inv_high, inv_high, inv_low], 0),
        np.concatenate([last_tok[0], last_tok[0], last_tok[1]], 1),
        np.concatenate([last_lag[0], last_lag[0], last_lag[1]], 1),
        twist,
    )


def dot(a, b):
    return jnp.dot(a, b, preferred_element_type=jnp.float32)


def split(x):
    high = x.astype(jnp.bfloat16)
    low = (x - high.astype(jnp.float32)).astype(jnp.bfloat16)
    return high, low


def forward(signal, first, second, twist):
    n, width = signal.shape[0], signal.shape[1] // 2
    part = dot(first, jnp.concatenate([signal, signal], 0))
    out = []
    for half in range(2):
        lanes = slice(half * width, (half + 1) * width)
        re, im = part[:n, lanes], part[n:, lanes]
        turned = jnp.concatenate(
            [re * twist[0] + im * twist[1], im * twist[0] - re * twist[1]], 1
        )
        high, low = split(turned)
        spec = dot(jnp.concatenate([high, low, high], 1), second)
        out.append((spec[:, :width], spec[:, width:]))
    return out


def inverse(spectra, second, last, twist):
    cols = []
    for re, im in spectra:
        width = re.shape[1]
        high, low = split(jnp.concatenate([re, im], 1))
        rot = dot(jnp.concatenate([high, low, high], 1), second)
        re, im = rot[:, :width], rot[:, width:]
        cols.append(
            jnp.concatenate([re * twist[0] - im * twist[1], im * twist[0] + re * twist[1]], 0)
        )
    high, low = split(jnp.concatenate(cols, 1))
    return dot(last, jnp.concatenate([high, low, high], 0))


def times(a, b):
    return [(ar * br - ai * bi, ar * bi + ai * br) for (ar, ai), (br, bi) in zip(a, b)]


def times_conj(a, b):
    return [(ar * br + ai * bi, ai * br - ar * bi) for (ar, ai), (br, bi) in zip(a, b)]


def pack_tokens(landed):
    blocks, _, width = landed.shape
    wide = landed.astype(jnp.float32)
    sides = [wide[:, h * HALF : (h + 1) * HALF, :].reshape(blocks * HALF, width) for h in range(2)]
    return jnp.concatenate(sides, 1).astype(jnp.bfloat16)


def unpack_tokens(cols, blocks):
    width = cols.shape[1] // 2
    sides = [cols[:, h * width : (h + 1) * width].reshape(blocks, HALF, width) for h in range(2)]
    return jnp.concatenate(sides, 1).astype(jnp.bfloat16)


def along(me, step):
    side = (step + 1) // 2
    return (me + 8 + side - 2 * side * ((step + 1) % 2)) % ROW


def kernel(
    go_hbm, q_hbm, k_hbm, v_hbm, f_hbm,
    first_tok_hbm, first_filt_hbm, fwd_hbm, inv_hbm, last_tok_hbm, last_lag_hbm, twist_hbm,
    conv_in, back_in, lag_in,
    go, q, k, v, f_row,
    first_tok, first_filt, fwd, inv, last_tok, last_lag, twist,
    g_out, m_out, g_in, m_in, f_wide, f_out, f_in,
    back_out, conv_out, lag_out,
    load_sem, table_sem, send_sem, recv_sem, row_sem,
):
    me, dp = lax.axis_index("ctx"), lax.axis_index("dp")
    n_ctx, n_dp = g_out.shape[0], f_in.shape[0]
    loads = [
        pltpu.make_async_copy(src, dst, load_sem.at[i])
        for i, (src, dst) in enumerate([(go_hbm, go), (q_hbm, q), (k_hbm, k), (v_hbm, v), (f_hbm, f_row)])
    ]
    barrier = pltpu.get_barrier_semaphore()

    row = me // ROW

    def greet(sem, z, x):
        pl.semaphore_signal(sem, inc=1, device_id=(dp, x * ROW + z), device_id_type=MESH)

    for step in range(ROW - 1):
        greet(barrier, along(me, step), row)

    for step in range(1, n_dp):
        pl.semaphore_signal(
            barrier, inc=1, device_id=((dp + step) % n_dp, me), device_id_type=MESH
        )
    for load in loads:
        load.start()
    tables = [
        pltpu.make_async_copy(src, dst, table_sem.at[i])
        for i, (src, dst) in enumerate(
            [
                (first_filt_hbm, first_filt),
                (twist_hbm, twist),
                (fwd_hbm, fwd),
                (first_tok_hbm, first_tok),
                (inv_hbm, inv),
                (last_tok_hbm, last_tok),
                (last_lag_hbm, last_lag),
            ]
        )
    ]
    for table in tables:
        table.start()

    def product(a, b):
        wide = a[0].astype(jnp.float32) * b[0].astype(jnp.float32)
        return wide.T.astype(jnp.bfloat16).reshape(g_out.shape)

    loads[0].wait()
    loads[1].wait()
    g_out[...] = product(go, q)
    blocks, width = f_out.shape
    pl.semaphore_wait(barrier, ROW - 1 + n_dp - 1 + row)

    @pl.when(row == 0)
    def _():
        greet(barrier, me % ROW, 1)

    @pl.when(row == 1)
    def _():
        greet(row_sem, me % ROW, 0)

    def send_one(src, dst, which, to, z):
        peer = to * ROW + z
        pltpu.make_async_remote_copy(
            src_ref=src.at[peer],
            dst_ref=dst.at[me],
            send_sem=send_sem.at[which],
            recv_sem=recv_sem.at[which],
            device_id=(dp, peer),
            device_id_type=MESH,
        ).start()

    def send_same(src, dst, which):
        for step in range(ROW - 1):
            send_one(src, dst, which, row, along(me, step))

    def send_cross(src, dst, which):
        for step in range(ROW):
            send_one(src, dst, which, 1 - row, along(me, step))

    def send_both(src, dst, which, first=1):
        for step in range(ROW):
            for flip in (first, 1 - first):
                if flip or step < ROW - 1:
                    send_one(src, dst, which, (row + flip) % 2, along(me, step))

    def keep(src, dst, which):
        pltpu.make_async_copy(src.at[me], dst.at[me], recv_sem.at[which]).start()

    def send_dp(pick, dst, which):
        def body(step, carry):
            peer = (dp + step) % n_dp
            pltpu.make_async_remote_copy(
                src_ref=pick(peer),
                dst_ref=dst.at[dp],
                send_sem=send_sem.at[which],
                recv_sem=recv_sem.at[which],
                device_id=(peer, me),
                device_id_type=MESH,
            ).start()
            return carry

        lax.fori_loop(1, n_dp, body, 0, unroll=True)
        pltpu.make_async_copy(pick(dp), dst.at[dp], recv_sem.at[which]).start()

    def landed(dst, which):
        pltpu.make_async_copy(dst, dst, recv_sem.at[which]).wait()

    def sent(dst, which):
        rest = dst.at[pl.ds(0, dst.shape[0] - 1)]
        pltpu.make_async_copy(rest, rest, send_sem.at[which]).wait()

    keep(g_out, g_in, 0)

    @pl.when(row == 0)
    def _():
        send_same(g_out, g_in, 0)
        pl.semaphore_wait(row_sem, 1)
        send_cross(g_out, g_in, 0)

    @pl.when(row == 1)
    def _():
        send_cross(g_out, g_in, 0)
        send_same(g_out, g_in, 0)

    loads[2].wait()
    loads[3].wait()
    m_out[...] = product(k, v)
    keep(m_out, m_in, 2)
    send_both(m_out, m_in, 2)
    loads[4].wait()
    taps = f_row[...].astype(jnp.float32)
    for i in range(blocks):
        f_wide[pl.ds(i, 1), :] = taps[:, i * width : (i + 1) * width]
    f_out[...] = f_wide[...].astype(jnp.bfloat16)
    send_dp(lambda peer: f_out, f_in, 1)
    for table in tables:
        table.wait()
    landed(f_in, 1)
    filt = jnp.concatenate(
        [f_in[h * HALF : (h + 1) * HALF].reshape(HALF * blocks, width) for h in range(2)], 1
    )
    filt_spec = forward(filt, first_filt[...], fwd[...], twist)
    landed(g_in, 0)
    grad_spec = forward(pack_tokens(g_in[...]), first_tok[...], fwd[...], twist)
    back_cols = inverse(times_conj(grad_spec, filt_spec), inv[...], last_tok[...], twist)
    back_out[...] = unpack_tokens(back_cols, blocks)
    keep(back_out, back_in, 3)
    send_both(back_out, back_in, 3)
    landed(m_in, 2)
    mixed_spec = forward(pack_tokens(m_in[...]), first_tok[...], fwd[...], twist)
    conv_cols = inverse(times(mixed_spec, filt_spec), inv[...], last_tok[...], twist)
    conv_out[...] = unpack_tokens(conv_cols, blocks)
    keep(conv_out, conv_in, 4)

    @pl.when(row == 0)
    def _():
        send_both(conv_out, conv_in, 4)

    @pl.when(row == 1)
    def _():
        send_cross(conv_out, conv_in, 4)
        send_same(conv_out, conv_in, 4)
    lag_cols = inverse(times_conj(grad_spec, mixed_spec), inv[...], last_lag[...], twist)
    for h in range(2):
        lag_out[h * HALF : (h + 1) * HALF] = (
            lag_cols[:, h * width : (h + 1) * width]
            .reshape(HALF, blocks, width)
            .astype(jnp.bfloat16)
        )
    send_dp(lambda peer: lag_out.at[peer], lag_in, 5)

    landed(back_in, 3)
    landed(lag_in, 5)
    landed(conv_in, 4)
    for which, dst in enumerate([g_in, f_in, m_in, back_in, conv_in, lag_in]):
        sent(dst, which)


def gate(
    scale,
    conv_hbm, back_hbm, lag_hbm, go_hbm, k_hbm, v_hbm,
    gq_hbm, gk_hbm, gv_hbm, gf_hbm,
    conv, back, lag, go, k, v, gq, gk, gv, gf,
    load_sem, store_sem,
):
    loads = [
        pltpu.make_async_copy(src, dst, load_sem.at[i])
        for i, (src, dst) in enumerate(
            [(back_hbm, back), (v_hbm, v), (k_hbm, k), (conv_hbm, conv), (go_hbm, go), (lag_hbm, lag)]
        )
    ]
    stores = [
        pltpu.make_async_copy(src, dst, store_sem.at[i])
        for i, (src, dst) in enumerate([(gk, gk_hbm), (gv, gv_hbm), (gq, gq_hbm), (gf, gf_hbm)])
    ]
    for load in loads:
        load.start()
    channels, width = go.shape[2], go.shape[1]

    def rows(arrived):
        return arrived[...].astype(jnp.float32).reshape(channels, width).T

    loads[0].wait()
    cols = rows(back)
    loads[1].wait()
    gk[0] = (cols * v[0].astype(jnp.float32)).astype(jnp.bfloat16)
    stores[0].start()
    loads[2].wait()
    gv[0] = (cols * k[0].astype(jnp.float32)).astype(jnp.bfloat16)
    stores[1].start()
    loads[3].wait()
    loads[4].wait()
    gq[0] = (rows(conv) * go[0].astype(jnp.float32)).astype(jnp.bfloat16)
    stores[2].start()
    loads[5].wait()
    gf[...] = jnp.sum(lag[...].astype(jnp.float32), axis=0) * scale
    stores[3].start()
    for done in stores:
        done.wait()


def per_device(grad_out, query_proj, key_proj, value_proj, filters):
    n_ctx, n_dp = lax.axis_size("ctx"), lax.axis_size("dp")
    _, width, channels = grad_out.shape
    blocks = n_ctx
    own = channels // n_ctx
    assert own == n_dp == 2 * HALF and filters.shape == (1, blocks * width)
    tables = make_tables(blocks, width)
    scale = 1.0 / math.sqrt(grad_out.shape[0] * n_dp * n_ctx * width)
    vmem = pl.BlockSpec(memory_space=pltpu.VMEM)
    hbm = pl.BlockSpec(memory_space=pltpu.HBM)
    bf16, f32 = jnp.bfloat16, jnp.float32
    tok = grad_out.shape
    cols = pltpu.VMEM((n_ctx, own, width), bf16)
    rows = pltpu.VMEM((n_dp, blocks, width), bf16)
    outs = pl.pallas_call(
        kernel,
        out_shape=[
            jax.ShapeDtypeStruct((n_ctx, own, width), bf16),
            jax.ShapeDtypeStruct((n_ctx, own, width), bf16),
            jax.ShapeDtypeStruct((n_dp, blocks, width), bf16),
        ],
        in_specs=[hbm] * (5 + len(tables)),
        out_specs=[hbm] * 3,
        scratch_shapes=[pltpu.VMEM(tok, bf16)] * 4
        + [pltpu.VMEM(filters.shape, bf16)]
        + [pltpu.VMEM(t.shape, t.dtype) for t in tables]
        + [cols] * 4
        + [pltpu.VMEM((blocks, width), f32), pltpu.VMEM((blocks, width), bf16), rows]
        + [cols] * 2
        + [rows]
        + [
            pltpu.SemaphoreType.DMA((5,)),
            pltpu.SemaphoreType.DMA((len(tables),)),
            pltpu.SemaphoreType.DMA((6,)),
            pltpu.SemaphoreType.DMA((6,)),
            pltpu.SemaphoreType.REGULAR,
        ],
        compiler_params=pltpu.CompilerParams(
            collective_id=0, has_side_effects=True, vmem_limit_bytes=63 * 1024 * 1024
        ),
        name="hyena_backward",
    )(grad_out, query_proj, key_proj, value_proj, filters, *[jnp.asarray(t) for t in tables])
    outs = pl.pallas_call(
        functools.partial(gate, scale),
        out_shape=[jax.ShapeDtypeStruct(tok, bf16)] * 3
        + [jax.ShapeDtypeStruct((blocks, width), f32)],
        in_specs=[hbm] * 6,
        out_specs=[hbm] * 4,
        scratch_shapes=[cols, cols, rows]
        + [pltpu.VMEM(tok, bf16)] * 6
        + [
            pltpu.VMEM((blocks, width), f32),
            pltpu.SemaphoreType.DMA((6,)),
            pltpu.SemaphoreType.DMA((4,)),
        ],
        compiler_params=pltpu.CompilerParams(vmem_limit_bytes=63 * 1024 * 1024),
        name="gate_outputs",
    )(outs[0], outs[1], outs[2], grad_out, key_proj, value_proj)
    return (*outs[:3], outs[3].reshape(filters.shape))


def solution(mesh):
    tokens, channels = P("dp", "ctx", None), P(("ctx", "dp"), None)
    return jax.shard_map(
        per_device,
        mesh=mesh,
        in_specs=(tokens, tokens, tokens, tokens, channels),
        out_specs=(tokens, tokens, tokens, channels),
        check_vma=False,
    )
```
